32 devices in a mesh: seq: 2 (over x), exp: 8 (over z, core), head: 2 (over y).
Axes of the slice: x: 2, y: 2, z: 4, core: 2. Of those that a mesh axis runs over, the one named last changes fastest.
Arguments:
- out_grad: bfloat16 [768, 2048], P(('exp', 'head')), may hold values from -6 to 6
- layer_input: bfloat16 [768, 2048], P(('exp', 'head')), may hold values from -6 to 6
- norm_gain: float32 [2048], replicated, may hold values from 0.5 to 1.5
- routes: int32 [768, 8], P(('exp', 'head')), may hold values from 0 to 15, all different within a row; in each aligned block of 48 rows (0 to 47, 48 to 95, ...) at most 32 rows name the same one
- gates: float32 [768, 8], P(('exp', 'head')), may hold values from 0.02 to 0.3
- gate_pre: bfloat16 [2, 16, 8, 32, 768], P('head', 'exp', None, None, 'seq'), may hold values from -6 to 6
- up_pre: bfloat16 [2, 16, 8, 32, 768], P('head', 'exp', None, None, 'seq'), may hold values from -6 to 6
- w_gate: bfloat16 [16, 2048, 768], P('exp', None, 'seq'), may hold values from -0.125 to 0.125
- w_up: bfloat16 [16, 2048, 768], P('exp', None, 'seq'), may hold values from -0.125 to 0.125
- w_down: bfloat16 [16, 768, 2048], P('exp', 'seq'), may hold values from -0.21875 to 0.21875
- w_out: bfloat16 [4096, 2048], P('head'), may hold values from -0.09375 to 0.09375
Outputs:
- resid_grad: float32 [2, 384, 2048], P('seq', ('exp', 'head'))
- head_grad: bfloat16 [2, 384, 4096], P('seq', 'exp', 'head')
The draws below stay inside these ranges and needn't reach their ends.
Inputs may be any that keep to these rules, and one draw needn't show every extreme that they name: `routes`: each row names 8 different experts. In each aligned block of 48 rows (the tokens of one device) no expert is named by more than 32 rows, a bound that some block reaches.
All inputs are finite; a program needn't handle non-finite values.
Results may differ from the reference program's by a relative error of at most 0.0095.
Values may be sent and summed in bfloat16 or wider, within the bound.
A program may use at most 64 MiB of HBM per device.

```python
import math
import jax
import jax.numpy as jnp
import numpy as np
from jax import lax

D = 2048
FF = 768
TOPK = 8
TOK_DEV = 48
EXPERTS = 16
CAP = 32
ATTN = 4096
SEQ_GROUPS = 2
EXP_GROUPS = 8
HEAD_GROUPS = 2
TOKENS = 768


def levels(key, extent, cuts, low, top_value):
    gain = 1.0
    for dim, parts in cuts:
        heights = jax.random.uniform(jax.random.fold_in(jax.random.fold_in(key, 6), dim), (parts,), jnp.float32, low / len(cuts), top_value / len(cuts))
        gain = gain * jnp.repeat(jnp.exp(heights), extent[dim] // parts).reshape((-1,) + (1,) * (len(extent) - 1 - dim))
    return gain


def shared_out(rng, own, number, rows, number_of, top, most, slope):
    order = jax.random.permutation(rng, number_of)
    heavy_load, ordinary = shares(number_of, rows * top, most, slope, True), shares(number_of, rows * top, most, slope, False)
    places = jnp.arange(number_of)

    def named(lengths, turn):
        used = int((lengths > 0).sum())
        fixed = max(1, used // 4)
        passed = fixed + (places - fixed + turn * (used - fixed)) % max(1, number_of - fixed)
        return jnp.zeros((number_of,), jnp.int32).at[order[jnp.where(places < fixed, places, passed)]].set(jnp.asarray(lengths, jnp.int32))

    lengths = jnp.where(number % 4 == 0, named(heavy_load, number // 4), named(ordinary, number - number // 4 - 1))
    mixed = jax.random.permutation(jax.random.fold_in(own, 3), number_of)
    giver, sink = mixed[0:number_of // 2 * 2:2], mixed[1:number_of // 2 * 2:2]
    room = jnp.minimum(lengths[giver] - 1, most - lengths[sink]) // 2
    room = jnp.where((giver == order[0]) | (sink == order[0]) | (lengths[sink] == 0), 0, jnp.maximum(room, 0))
    passed = jax.random.randint(jax.random.fold_in(own, 4), (number_of // 2,), 0, 1 << 20) % (room + 1)
    lengths = lengths.at[giver].add(-passed).at[sink].add(passed)
    items = jnp.searchsorted(jnp.cumsum(lengths), jnp.arange(rows * top), side="right").astype(jnp.int32)
    table = items.reshape(top, rows).T
    table = table[jax.random.permutation(jax.random.fold_in(own, 1), rows)]
    turn = jax.random.randint(jax.random.fold_in(own, 2), (rows, 1), 0, top)
    return jnp.take_along_axis(table, (jnp.arange(top)[None, :] + turn) % top, axis=1)


def shares(amount, total, bound, skew, full):
    loads = [(1 << 20) // math.isqrt(grade ** skew) + 1 for grade in range(1, amount + 1)]
    largest = bound if full else min(bound, max(-(-total // amount), total * loads[0] // sum(loads)))
    least = 1 if total - largest >= amount - 1 else 0
    counts, surplus = [largest] + [least] * (amount - 1), total - largest - least * (amount - 1)
    while surplus > 0:
        movable = [i for i in range(1, amount) if counts[i] < largest] or [i for i in range(1, amount) if counts[i] < bound]
        mass, left = sum([loads[i] for i in movable]), surplus
        for i in movable:
            extra = min(bound - counts[i], max(1, left * loads[i] // mass), surplus)
            counts[i] = counts[i] + extra
            surplus = surplus - extra
    return np.array(counts)


def normal_values(rng, extent, deviation, reach, split=(), kind=jnp.bfloat16):
    result = jax.random.normal(rng, extent, jnp.float32) * deviation
    if len(split) > 0:
        result = levels(rng, extent, split, -0.22, 0.18) * result
    return jnp.clip(result, min=-reach, max=reach).astype(kind)


def setup_inputs(seed: int = 0) -> dict:
    key_of = jax.random.split(jax.random.key(seed), 12)
    out_grad = normal_values(key_of[0], (TOKENS, D), 1.0, 6.0, ((0, 16),))
    layer_input = normal_values(key_of[1], (TOKENS, D), 1.0, 6.0, ((0, 16),))
    norm_gain = jnp.clip(1.0 + 0.1 * jax.random.normal(key_of[2], (D,), jnp.float32), 0.5, 1.5)
    routes_keys = jax.random.split(jax.random.fold_in(key_of[3], 1), TOKENS // TOK_DEV)
    routes_turns = jax.random.permutation(jax.random.fold_in(key_of[3], 3), TOKENS // TOK_DEV)
    routes = jax.vmap(lambda own, number: shared_out(jax.random.fold_in(key_of[3], 2), own, number, TOK_DEV, EXPERTS, TOPK, CAP, 2))(routes_keys, routes_turns).reshape((TOKENS, TOPK))
    gates = jnp.clip(0.02 + 0.28 * jax.random.uniform(key_of[4], (TOKENS, TOPK), jnp.float32) ** levels(key_of[4], (TOKENS, TOPK), ((0, 16),), -0.2, 0.2), 0.02, 0.3)
    gate_pre = normal_values(key_of[5], (HEAD_GROUPS, EXPERTS, EXP_GROUPS, CAP, FF), 1.0, 6.0, ((0, 2), (1, 8), (4, 2)))
    up_pre = normal_values(key_of[6], (HEAD_GROUPS, EXPERTS, EXP_GROUPS, CAP, FF), 1.0, 6.0, ((0, 2), (1, 8), (4, 2)))
    w_gate = normal_values(key_of[7], (EXPERTS, D, FF), D ** -0.5, 0.125, ((0, 8), (2, 2)))
    w_up = normal_values(key_of[8], (EXPERTS, D, FF), D ** -0.5, 0.125, ((0, 8), (2, 2)))
    w_down = normal_values(key_of[9], (EXPERTS, FF, D), FF ** -0.5, 0.21875, ((0, 8), (1, 2)))
    w_out = normal_values(key_of[10], (ATTN, D), ATTN ** -0.5, 0.09375, ((0, 2),))
    return {"out_grad": out_grad, "layer_input": layer_input, "norm_gain": norm_gain, "routes": routes, "gates": gates, "gate_pre": gate_pre, "up_pre": up_pre, "w_gate": w_gate, "w_up": w_up, "w_down": w_down, "w_out": w_out}


def reference(out_grad, layer_input, norm_gain, routes, gates, gate_pre, up_pre, w_gate, w_up, w_down, w_out):
    block_count = HEAD_GROUPS * EXP_GROUPS
    expert_ids = jnp.arange(EXPERTS, dtype=jnp.int32)
    block_routes = routes.reshape(block_count, TOK_DEV * TOPK)
    onehot = (block_routes[:, :, None] == expert_ids[None, None, :]).astype(jnp.int32)
    position = lax.optimization_barrier(jnp.sum((jnp.cumsum(onehot, axis=1) - 1) * onehot, axis=2)).reshape(TOKENS, TOPK)
    block_id = jnp.arange(TOKENS, dtype=jnp.int32) // TOK_DEV
    source_exp = block_id // HEAD_GROUPS
    source_head = block_id % HEAD_GROUPS
    buffer_row = ((source_head * EXP_GROUPS + source_exp)[:, None] * CAP + position).astype(jnp.int32)
    grad_wide = out_grad.astype(jnp.float32)
    slot_total = HEAD_GROUPS * EXP_GROUPS * CAP
    quarter_ff = FF // SEQ_GROUPS

    def one_expert(carry, expert):
        chosen = routes == expert
        valid = jnp.any(chosen, axis=1)
        row_index = lax.optimization_barrier(jnp.sum(jnp.where(chosen, buffer_row, 0), axis=1)).astype(jnp.int32)
        weight = lax.optimization_barrier(jnp.sum(jnp.where(chosen, gates, 0.0), axis=1))
        scaled = (weight[:, None] * grad_wide).astype(jnp.bfloat16)
        target = jnp.where(valid, row_index, slot_total).astype(jnp.int32)
        slot_rows = jnp.zeros((slot_total, D), jnp.bfloat16).at[target].set(scaled, mode='drop')
        gate_act = lax.dynamic_index_in_dim(gate_pre, expert, 1, keepdims=False).reshape(slot_total, FF).astype(jnp.float32)
        up_act = lax.dynamic_index_in_dim(up_pre, expert, 1, keepdims=False).reshape(slot_total, FF).astype(jnp.float32)
        down_here = lax.dynamic_index_in_dim(w_down, expert, 0, keepdims=False)
        gate_here = lax.dynamic_index_in_dim(w_gate, expert, 0, keepdims=False)
        up_here = lax.dynamic_index_in_dim(w_up, expert, 0, keepdims=False)
        d_hidden = jnp.dot(slot_rows, down_here.T, preferred_element_type=jnp.float32)
        sigmoid_gate = jax.nn.sigmoid(gate_act)
        silu_gate = gate_act * sigmoid_gate
        silu_slope = sigmoid_gate * (1.0 + gate_act * (1.0 - sigmoid_gate))
        d_gate = (d_hidden * up_act * silu_slope).astype(jnp.bfloat16)
        d_up = (d_hidden * silu_gate).astype(jnp.bfloat16)
        gate_part = d_gate.astype(jnp.float32).reshape(slot_total, SEQ_GROUPS, quarter_ff)
        up_part = d_up.astype(jnp.float32).reshape(slot_total, SEQ_GROUPS, quarter_ff)
        gate_cols = gate_here.astype(jnp.float32).reshape(D, SEQ_GROUPS, quarter_ff)
        up_cols = up_here.astype(jnp.float32).reshape(D, SEQ_GROUPS, quarter_ff)
        quarters = jnp.einsum('rqf,dqf->qrd', gate_part, gate_cols) + jnp.einsum('rqf,dqf->qrd', up_part, up_cols)
        rounded = lax.optimization_barrier(quarters.astype(jnp.bfloat16))
        slot_part = lax.optimization_barrier(jnp.sum(rounded.astype(jnp.float32), axis=0))
        picked = slot_part[row_index]
        carry = carry + jnp.where(valid[:, None], picked, 0.0)
        return (carry, None)
    moe_grad, unused = lax.scan(one_expert, jnp.zeros((TOKENS, D), jnp.float32), expert_ids)
    inputs = layer_input.astype(jnp.float32)
    inv_rms = lax.rsqrt(lax.optimization_barrier(jnp.mean(inputs * inputs, axis=1, keepdims=True)) + 1e-06)
    normed = inputs * inv_rms
    scaled_grad = moe_grad * norm_gain[None, :]
    full_grad = grad_wide + inv_rms * (scaled_grad - normed * lax.optimization_barrier(jnp.mean(scaled_grad * normed, axis=1, keepdims=True)))
    head_full = jnp.dot(full_grad.astype(jnp.bfloat16), w_out.T, preferred_element_type=jnp.float32).astype(jnp.bfloat16)

    def arrange(values):
        shaped = values.reshape(block_count, SEQ_GROUPS, TOK_DEV // SEQ_GROUPS, values.shape[1])
        return shaped.transpose(1, 0, 2, 3).reshape(SEQ_GROUPS, TOKENS // SEQ_GROUPS, values.shape[1])
    return (arrange(full_grad), arrange(head_full))
```

```python
import functools

import jax
import jax.numpy as jnp
from jax import lax
from jax.experimental import pallas as pl
from jax.experimental.pallas import tpu as pltpu
from jax.sharding import PartitionSpec as P

MESH = pl.DeviceIdType.MESH
F32 = jnp.float32
BF16 = jnp.bfloat16
NT_DIMS = (((1,), (1,)), ((), ()))
COLUMN_TILES = 4


def dot_nt(a, b):
    return lax.dot_general(a, b, NT_DIMS, preferred_element_type=F32)


def kernel(
    sizes,
    og, li, gain, routes, gates, gp_hbm, up_hbm, wg_hbm, wu_hbm, wd_hbm, wo_hbm,
    resid, head,
    xg, info_src, info_all, gp, up, wg, wu, wd, wo, coef_gate, coef_up, dgate, dup,
    mine, core_rx, sx, x_rx, sz, z_rx, moe, hx, lhs,
    load_sem, z_snd, sib_snd, x_snd, info_snd, core_snd, xs_snd, zs_snd, head_snd,
    xg_rcv, info_rcv, core_rcv, xs_rcv, zs_rcv, head_rcv,
):
    S, E, H, J, T, D, C = sizes
    Z = E // 2
    DS = D // S
    R = T // S
    NT = COLUMN_TILES
    TN = DS // NT
    s = lax.axis_index("seq")
    e = lax.axis_index("exp")
    h = lax.axis_index("head")
    z = e // 2
    c = e % 2
    sib = z * 2 + (1 - c)

    def remote(src, dst, snd, rcv, **where):
        return pltpu.make_async_remote_copy(
            src_ref=src, dst_ref=dst, send_sem=snd, recv_sem=rcv,
            device_id=where, device_id_type=MESH,
        )

    barrier = pltpu.get_barrier_semaphore()
    for k in range(1, E):
        pl.semaphore_signal(barrier, inc=1, device_id={"exp": (e + k) % E}, device_id_type=MESH)
    for k in range(1, S):
        pl.semaphore_signal(barrier, inc=1, device_id={"seq": (s + k) % S}, device_id_type=MESH)
    for k in range(1, H):
        pl.semaphore_signal(barrier, inc=1, device_id={"head": (h + k) % H}, device_id_type=MESH)

    loads = [
        pltpu.make_async_copy(src, dst, load_sem.at[i])
        for i, (src, dst) in enumerate(
            ((gp_hbm, gp), (up_hbm, up), (wd_hbm, wd), (wg_hbm, wg), (wu_hbm, wu), (wo_hbm, wo))
        )
    ]
    for load in loads:
        load.start()
    for q in range(S):
        xg[e, q] = og[:, q * DS:(q + 1) * DS]

    pl.semaphore_wait(barrier, E - 1 + S - 1 + H - 1)

    sent = []

    def start(copy):
        copy.start()
        sent.append(copy)

    def chunk(block, part, snd, **where):
        return remote(xg.at[block, part], xg.at[block, part], snd, xg_rcv.at[block, part], **where)

    for k in range(1, Z):
        start(chunk(e, s, z_snd.at[k], exp=((z + k) % Z) * 2 + c))
    for q in range(S):
        start(chunk(e, q, sib_snd.at[0, q], exp=sib))

    X8 = E * 8
    XP = max(128, X8)
    lane = lax.broadcasted_iota(jnp.int32, (T, XP), 1)
    kind = lane % 8
    expert = (lane // 8) * J + kind % J
    weight = jnp.zeros((T, XP), F32)
    member = jnp.zeros((T, XP), F32)
    for k in range(routes.shape[1]):
        hit = routes[:, k:k + 1] == expert
        weight = weight + jnp.where(hit, gates[:, k:k + 1], 0.0)
        member = jnp.where(hit, 1.0, member)
    earlier = (
        lax.broadcasted_iota(jnp.int32, (T, T), 0) > lax.broadcasted_iota(jnp.int32, (T, T), 1)
    ).astype(F32).astype(BF16)
    position = jnp.dot(earlier, member.astype(BF16), preferred_element_type=F32)
    info = jnp.where(kind < J, weight, jnp.where(member > 0.0, position, -1.0))
    info = jnp.concatenate([info, jnp.zeros((128 - T, XP), F32)], axis=0).T
    info_src[...] = info[:X8].reshape(E, 8, 128)
    for k in range(1, E):
        to = (e + k) % E
        start(remote(info_src.at[to], info_all.at[e], info_snd.at[k], info_rcv.at[e], exp=to))
    info_all[e] = info_src[e]

    for k in range(1, Z):
        block = ((z + k) % Z) * 2 + c
        chunk(block, s, z_snd.at[k], exp=sib).wait_recv()
        for i in range(1, S):
            start(chunk(block, s, x_snd.at[k, i], seq=(s + i) % S))
        start(chunk(block, s, sib_snd.at[k, 0], exp=sib))

    for k in range(1, E):
        frm = (e + k) % E
        remote(info_src.at[frm], info_all.at[frm], info_snd.at[k], info_rcv.at[frm], exp=frm).wait_recv()
    table = info_all[...].reshape(X8, 128)
    if XP > X8:
        table = jnp.concatenate([table, jnp.zeros((XP - X8, 128), F32)], axis=0)
    table = table.T
    loads[0].wait()
    loads[1].wait()
    slot = lax.broadcasted_iota(jnp.int32, (E * T, E * C), 1).astype(F32)
    for j in range(J):
        gate_col = jnp.concatenate([table[:T, b * 8 + j:b * 8 + j + 1] for b in range(E)], axis=0)
        place = []
        for b in range(E):
            col = table[:T, b * 8 + J + j:b * 8 + J + j + 1]
            place.append(jnp.where(col >= 0.0, col + float(b * C), -1.0))
        place = jnp.concatenate(place, axis=0)
        pick = jnp.where(slot == place, 1.0, 0.0).astype(BF16)
        a = jnp.dot(pick, gp[j], preferred_element_type=F32)
        b = jnp.dot(pick, up[j], preferred_element_type=F32)
        sig = jax.nn.sigmoid(a)
        coef_gate[j] = gate_col * b * sig * (1.0 + a * (1.0 - sig))
        coef_up[j] = gate_col * a * sig

    for k in range(1, Z):
        block = ((z + k) % Z) * 2 + c
        for i in range(1, S):
            part = (s + S - i) % S
            chunk(block, part, x_snd.at[k, i], exp=sib).wait_recv()
            start(chunk(block, part, sib_snd.at[k, i], exp=sib))

    for k in range(Z):
        block = ((z + k) % Z) * 2 + (1 - c)
        for i in range(S):
            part = (s + S - i) % S
            chunk(block, part, sib_snd.at[k, i], exp=sib).wait_recv()

    loads[2].wait()
    for j in range(J):
        hidden = None
        for q in range(S):
            term = dot_nt(xg[:, q].reshape(E * T, DS), wd[j, :, q * DS:(q + 1) * DS])
            hidden = term if hidden is None else hidden + term
        dgate[j] = (hidden * coef_gate[j]).astype(BF16)
        dup[j] = (hidden * coef_up[j]).astype(BF16)
    loads[3].wait()
    loads[4].wait()

    def core_copy(n):
        return remote(mine.at[n, 1 - c], core_rx.at[n], core_snd.at[n], core_rcv.at[n], exp=sib)

    def x_copy(n, i):
        to = (s + i) % S
        return remote(sx.at[n, to], x_rx.at[n, i], xs_snd.at[n, i], xs_rcv.at[n, i], seq=to)

    def z_copy(n, k):
        to = (z + k) % Z
        return remote(sz.at[n, to], z_rx.at[n, k], zs_snd.at[n, k], zs_rcv.at[n, k], exp=to * 2 + c)

    def stage_compute(n):
        tiles = []
        for q in range(S):
            cols = slice(q * DS + n * TN, q * DS + (n + 1) * TN)
            acc = None
            for j in range(J):
                term = dot_nt(dgate[j], wg[j, cols, :]) + dot_nt(dup[j], wu[j, cols, :])
                acc = term if acc is None else acc + term
            tiles.append(acc)
        for b in range(E):
            for p in range(S):
                rows = slice(b * T + p * R, b * T + (p + 1) * R)
                mine[n, b % 2, p, b // 2] = jnp.concatenate(
                    [tile[rows] for tile in tiles], axis=0
                ).astype(BF16)
        start(core_copy(n))

    def stage_x(n):
        core_copy(n).wait_recv()
        sx[n] = (mine[n, c].astype(F32) + core_rx[n].astype(F32)).astype(BF16)
        for i in range(1, S):
            start(x_copy(n, i))

    def stage_z(n):
        total = sx[n, s].astype(F32)
        for i in range(1, S):
            x_copy(n, i).wait_recv()
            total = total + x_rx[n, i].astype(F32)
        sz[n] = total.astype(BF16)
        for k in range(1, Z):
            start(z_copy(n, k))

    def stage_end(n):
        total = sz[n, z].astype(F32)
        for k in range(1, Z):
            z_copy(n, k).wait_recv()
            total = total + z_rx[n, k].astype(F32)
        for q in range(S):
            moe[:, q * DS + n * TN:q * DS + (n + 1) * TN] = total[q * R:(q + 1) * R]

    stages = (stage_compute, stage_x, stage_z, stage_end)
    for step in range(NT + len(stages) - 1):
        for i, stage in enumerate(stages):
            if 0 <= step - i < NT:
                stage(step - i)

    def rows_of(ref):
        wide = ref[...].astype(F32)
        mine_rows = wide[:R]
        for p in range(1, S):
            mine_rows = jnp.where(s == p, wide[p * R:(p + 1) * R], mine_rows)
        return mine_rows

    inputs = rows_of(li)
    inv_rms = lax.rsqrt(jnp.mean(inputs * inputs, axis=1, keepdims=True) + 1e-06)
    normed = inputs * inv_rms
    scaled = moe[...] * gain[...]
    full = rows_of(og) + inv_rms * (
        scaled - normed * jnp.mean(scaled * normed, axis=1, keepdims=True)
    )
    resid[...] = full
    hx[h] = jnp.concatenate([full[:, q * DS:(q + 1) * DS] for q in range(S)], axis=0).astype(BF16)
    for k in range(1, H):
        start(remote(hx.at[h], hx.at[h], head_snd.at[k], head_rcv.at[h], head=(h + k) % H))
    for k in range(1, H):
        frm = (h + k) % H
        remote(hx.at[frm], hx.at[frm], head_snd.at[k], head_rcv.at[frm], head=frm).wait_recv()
    parts = [hx[p].astype(F32) for p in range(H)]
    for q in range(S):
        lhs[:, q * DS:(q + 1) * DS] = jnp.concatenate(
            [part[q * R:(q + 1) * R] for part in parts], axis=0
        ).astype(BF16)
    loads[5].wait()
    A = wo.shape[0]
    AT = min(A, 512)
    for a0 in range(0, A, AT):
        head[:, a0:a0 + AT] = dot_nt(lhs[...], wo[a0:a0 + AT, :]).astype(BF16)
    for copy in sent:
        copy.wait_send()


def shards(
    out_grad, layer_input, norm_gain, routes, gates, gate_pre, up_pre, w_gate, w_up, w_down, w_out
):
    S, E, H = lax.axis_size("seq"), lax.axis_size("exp"), lax.axis_size("head")
    T, D = out_grad.shape
    J, F = w_down.shape[:2]
    C = gate_pre.shape[3]
    A = w_out.shape[0]
    Z = E // 2
    DS = D // S
    R = T // S
    NT = COLUMN_TILES
    TN = DS // NT
    gp = gate_pre.reshape(J, E * C, F)
    up = up_pre.reshape(J, E * C, F)
    vmem = pl.BlockSpec(memory_space=pltpu.VMEM)
    hbm = pl.BlockSpec(memory_space=pl.ANY)
    dma = pltpu.SemaphoreType.DMA
    scratch = [
        pltpu.VMEM((E, S, T, DS), BF16),
        pltpu.VMEM((E, 8, 128), F32),
        pltpu.VMEM((E, 8, 128), F32),
        pltpu.VMEM((J, E * C, F), BF16),
        pltpu.VMEM((J, E * C, F), BF16),
        pltpu.VMEM((J, D, F), BF16),
        pltpu.VMEM((J, D, F), BF16),
        pltpu.VMEM((J, F, D), BF16),
        pltpu.VMEM((A, D), BF16),
        pltpu.VMEM((J, E * T, F), F32),
        pltpu.VMEM((J, E * T, F), F32),
        pltpu.VMEM((J, E * T, F), BF16),
        pltpu.VMEM((J, E * T, F), BF16),
        pltpu.VMEM((NT, 2, S, Z, T, TN), BF16),
        pltpu.VMEM((NT, S, Z, T, TN), BF16),
        pltpu.VMEM((NT, S, Z, T, TN), BF16),
        pltpu.VMEM((NT, S, Z, T, TN), BF16),
        pltpu.VMEM((NT, Z, T, TN), BF16),
        pltpu.VMEM((NT, Z, T, TN), BF16),
        pltpu.VMEM((R, D), F32),
        pltpu.VMEM((H, T, DS), BF16),
        pltpu.VMEM((H * R, D), BF16),
        dma((6,)), dma((Z,)), dma((Z, S)), dma((Z, S)), dma((E,)), dma((NT,)),
        dma((NT, S)), dma((NT, Z)), dma((H,)),
        dma((E, S)), dma((E,)), dma((NT,)), dma((NT, S)), dma((NT, Z)), dma((H,)),
    ]
    rows = E * T
    flops = 2 * rows * D * F * J * 3 + 2 * H * R * D * A
    resid, head = pl.pallas_call(
        functools.partial(kernel, (S, E, H, J, T, D, C)),
        out_shape=(
            jax.ShapeDtypeStruct((R, D), F32),
            jax.ShapeDtypeStruct((H * R, A), BF16),
        ),
        in_specs=[vmem] * 5 + [hbm] * 6,
        out_specs=(vmem, vmem),
        scratch_shapes=scratch,
        compiler_params=pltpu.CompilerParams(
            collective_id=0, has_side_effects=True, vmem_limit_bytes=56 * 1024 * 1024
        ),
        cost_estimate=pl.CostEstimate(
            flops=flops, bytes_accessed=2 * (3 * J * D * F + A * D), transcendentals=rows * F * J
        ),
    )(
        out_grad, layer_input, norm_gain[None, :], routes, gates, gp, up,
        w_gate, w_up, w_down, w_out,
    )
    return (resid[None], head[None])


def solution(mesh):
    placed = (
        P(("exp", "head"), None),
        P(("exp", "head"), None),
        P(),
        P(("exp", "head"), None),
        P(("exp", "head"), None),
        P("head", "exp", None, None, "seq"),
        P("head", "exp", None, None, "seq"),
        P("exp", None, "seq"),
        P("exp", None, "seq"),
        P("exp", "seq", None),
        P("head", None),
    )
    return jax.shard_map(
        shards,
        mesh=mesh,
        in_specs=placed,
        out_specs=(P("seq", ("exp", "head"), None), P("seq", "exp", "head")),
        check_vma=False,
    )
```

```python
import functools

import jax
import jax.numpy as jnp
from jax import lax
from jax.experimental import pallas as pl
from jax.experimental.pallas import tpu as pltpu
from jax.sharding import PartitionSpec as P

MESH = pl.DeviceIdType.MESH
F32 = jnp.float32
BF16 = jnp.bfloat16
NT_DIMS = (((1,), (1,)), ((), ()))
LANES = 128


def dot_nt(a, b):
    return lax.dot_general(a, b, NT_DIMS, preferred_element_type=F32)


def kernel(
    sizes,
    og, li, gain, routes, gates, gp_hbm, up_hbm, wg_hbm, wu_hbm, wd_hbm, wo_hbm,
    resid, head,
    xg, info_src, info_all, gp, up, wg, wu, wd, wo, coef_gate, coef_up, dgate, dup,
    mine, core_rx, sx, x_rx, sz, z_rx, moe, normed, hx, lhs,
    load_sem, z_snd, sib_snd, x_snd, info_snd, core_snd, xs_snd, zs_snd, head_snd,
    xg_rcv, info_rcv, core_rcv, xs_rcv, zs_rcv, head_rcv,
):
    S, E, H, J, T, D, C = sizes
    Z = E // 2
    DS = D // S
    R = T // S
    F = wd.shape[1]
    TN = LANES
    NT = DS // TN
    s = lax.axis_index("seq")
    e = lax.axis_index("exp")
    h = lax.axis_index("head")
    z = e // 2
    c = e % 2
    sib = z * 2 + (1 - c)

    def remote(src, dst, snd, rcv, **where):
        return pltpu.make_async_remote_copy(
            src_ref=src, dst_ref=dst, send_sem=snd, recv_sem=rcv,
            device_id=where, device_id_type=MESH,
        )

    def rows_of(ref):
        wide = ref[...].astype(F32)
        mine_rows = wide[:R]
        for p in range(1, S):
            mine_rows = jnp.where(s == p, wide[p * R:(p + 1) * R], mine_rows)
        return mine_rows

    barrier = pltpu.get_barrier_semaphore()
    for k in range(1, E):
        pl.semaphore_signal(barrier, inc=1, device_id={"exp": (e + k) % E}, device_id_type=MESH)
    for k in range(1, S):
        pl.semaphore_signal(barrier, inc=1, device_id={"seq": (s + k) % S}, device_id_type=MESH)
    for k in range(1, H):
        pl.semaphore_signal(barrier, inc=1, device_id={"head": (h + k) % H}, device_id_type=MESH)

    loads = [
        pltpu.make_async_copy(src, dst, load_sem.at[i])
        for i, (src, dst) in enumerate(
            ((gp_hbm, gp), (up_hbm, up), (wd_hbm, wd), (wg_hbm, wg), (wu_hbm, wu), (wo_hbm, wo))
        )
    ]
    for load in loads:
        load.start()
    for q in range(S):
        xg[e, q] = og[:, q * DS:(q + 1) * DS]

    X8 = E * 8
    XP = max(LANES, X8)
    line = lax.broadcasted_iota(jnp.int32, (X8, T), 0)
    kind = line % 8
    expert = (line // 8) * J + kind % J
    weight = jnp.zeros((X8, T), F32)
    member = jnp.zeros((X8, T), F32)
    for k in range(routes.shape[0]):
        hit = routes[k:k + 1, :] == expert
        weight = weight + jnp.where(hit, gates[k:k + 1, :], 0.0)
        member = jnp.where(hit, 1.0, member)
    earlier = (
        lax.broadcasted_iota(jnp.int32, (T, T), 0) < lax.broadcasted_iota(jnp.int32, (T, T), 1)
    ).astype(F32).astype(BF16)
    position = jnp.dot(member.astype(BF16), earlier, preferred_element_type=F32)
    info = jnp.where(kind < J, weight, jnp.where(member > 0.0, position, -1.0))
    info_src[...] = jnp.zeros((E, 8, LANES), F32)
    info_src[:, :, :T] = info.reshape(E, 8, T)
    info_all[e] = info_src[e]

    pl.semaphore_wait(barrier, E - 1 + S - 1 + H - 1)

    sent = []

    def start(copy):
        copy.start()
        sent.append(copy)

    def chunk(block, part, snd, **where):
        return remote(xg.at[block, part], xg.at[block, part], snd, xg_rcv.at[block, part], **where)

    for k in range(1, E):
        to = (e + k) % E
        start(remote(info_src.at[to], info_all.at[e], info_snd.at[k], info_rcv.at[e], exp=to))
    for k in range(1, Z):
        start(chunk(e, s, z_snd.at[k], exp=((z + k) % Z) * 2 + c))
    for q in range(S):
        start(chunk(e, q, sib_snd.at[0, q], exp=sib))

    inputs = rows_of(li)
    inv_rms = lax.rsqrt(jnp.mean(inputs * inputs, axis=1, keepdims=True) + 1e-06)
    normed[...] = inputs * inv_rms

    for k in range(1, E):
        frm = (e + k) % E
        remote(info_src.at[frm], info_all.at[frm], info_snd.at[k], info_rcv.at[frm], exp=frm).wait_recv()
    loads[0].wait()
    loads[1].wait()

    def slot_values(experts):
        table = info_all[...].reshape(X8, LANES)
        if XP > X8:
            table = jnp.concatenate([table, jnp.zeros((XP - X8, LANES), F32)], axis=0)
        table = table.T
        slot = lax.broadcasted_iota(jnp.int32, (E * T, E * C), 1).astype(F32)
        for j in experts:
            gate_col = jnp.concatenate([table[:T, b * 8 + j:b * 8 + j + 1] for b in range(E)], axis=0)
            place = []
            for b in range(E):
                col = table[:T, b * 8 + J + j:b * 8 + J + j + 1]
                place.append(jnp.where(col >= 0.0, col + float(b * C), -1.0))
            place = jnp.concatenate(place, axis=0)
            pick = jnp.where(slot == place, 1.0, 0.0).astype(BF16)
            a = jnp.dot(pick, gp[j], preferred_element_type=F32)
            b = jnp.dot(pick, up[j], preferred_element_type=F32)
            sig = jax.nn.sigmoid(a)
            coef_gate[j] = gate_col * b * sig * (1.0 + a * (1.0 - sig))
            coef_up[j] = gate_col * a * sig

    slot_values(range(1))

    for k in range(1, Z):
        block = ((z + k) % Z) * 2 + c
        chunk(block, s, z_snd.at[k], exp=sib).wait_recv()
        for i in range(1, S):
            start(chunk(block, s, x_snd.at[k, i], seq=(s + i) % S))
        start(chunk(block, s, sib_snd.at[k, 0], exp=sib))

    slot_values(range(1, J))

    for k in range(1, Z):
        block = ((z + k) % Z) * 2 + c
        for i in range(1, S):
            part = (s + S - i) % S
            chunk(block, part, x_snd.at[k, i], exp=sib).wait_recv()
            start(chunk(block, part, sib_snd.at[k, i], exp=sib))

    for k in range(Z):
        block = ((z + k) % Z) * 2 + (1 - c)
        for i in range(S):
            part = (s + S - i) % S
            chunk(block, part, sib_snd.at[k, i], exp=sib).wait_recv()

    loads[2].wait()
    hidden = None
    for q in range(S):
        down = wd[:, :, q * DS:(q + 1) * DS].reshape(J * F, DS)
        term = dot_nt(xg[:, q].reshape(E * T, DS), down)
        hidden = term if hidden is None else hidden + term
    for j in range(J):
        here = hidden[:, j * F:(j + 1) * F]
        dgate[j] = (here * coef_gate[j]).astype(BF16)
        dup[j] = (here * coef_up[j]).astype(BF16)
    loads[3].wait()
    loads[4].wait()

    def core_copy(n):
        return remote(mine.at[n, 1 - c], core_rx.at[n], core_snd.at[n], core_rcv.at[n], exp=sib)

    def x_copy(n, i):
        to = (s + i) % S
        return remote(sx.at[n, to], x_rx.at[n, i], xs_snd.at[n, i], xs_rcv.at[n, i], seq=to)

    def z_copy(n, k):
        to = (z + k) % Z
        return remote(sz.at[n, to], z_rx.at[n, k], zs_snd.at[n, k], zs_rcv.at[n, k], exp=to * 2 + c)

    def stage_compute(n):
        bands = [slice(q * DS + n * TN, q * DS + (n + 1) * TN) for q in range(S)]

        def weights(ref, j):
            return jnp.concatenate([ref[j, band, :] for band in bands], axis=0)

        left = [ref[j] for j in range(J) for ref in (dgate, dup)]
        right = [weights(ref, j) for j in range(J) for ref in (wg, wu)]
        if F % LANES == 0:
            acc = dot_nt(jnp.concatenate(left, axis=1), jnp.concatenate(right, axis=1))
        else:
            acc = sum(dot_nt(lt, rt) for lt, rt in zip(left, right))
        tiles = [acc[:, q * TN:(q + 1) * TN] for q in range(S)]
        for b in range(E):
            for p in range(S):
                rows = slice(b * T + p * R, b * T + (p + 1) * R)
                mine[n, b % 2, p, b // 2] = jnp.concatenate(
                    [tile[rows] for tile in tiles], axis=0
                ).astype(BF16)
        start(core_copy(n))

    def stage_x(n):
        core_copy(n).wait_recv()
        sx[n] = (mine[n, c].astype(F32) + core_rx[n].astype(F32)).astype(BF16)
        for i in range(1, S):
            start(x_copy(n, i))

    def stage_z(n):
        total = sx[n, s].astype(F32)
        for i in range(1, S):
            x_copy(n, i).wait_recv()
            total = total + x_rx[n, i].astype(F32)
        sz[n] = total.astype(BF16)
        for k in range(1, Z):
            start(z_copy(n, k))

    def stage_end(n):
        total = sz[n, z].astype(F32)
        for k in range(1, Z):
            z_copy(n, k).wait_recv()
            total = total + z_rx[n, k].astype(F32)
        for q in range(S):
            moe[:, q * DS + n * TN:q * DS + (n + 1) * TN] = total[q * R:(q + 1) * R]

    for n in range(NT):
        stage_compute(n)
        if n >= 1:
            stage_x(n - 1)
        if n >= 5:
            stage_z(n - 5)
    stage_x(NT - 1)
    for n in range(max(NT - 5, 0), NT):
        stage_z(n)
    for n in range(NT):
        stage_end(n)

    scaled = moe[...] * gain[...]
    full = rows_of(og) + inv_rms * (
        scaled - normed[...] * jnp.mean(scaled * normed[...], axis=1, keepdims=True)
    )
    resid[...] = full
    hx[h] = jnp.concatenate([full[:, q * DS:(q + 1) * DS] for q in range(S)], axis=0).astype(BF16)
    for k in range(1, H):
        start(remote(hx.at[h], hx.at[h], head_snd.at[k], head_rcv.at[h], head=(h + k) % H))
    for k in range(1, H):
        frm = (h + k) % H
        remote(hx.at[frm], hx.at[frm], head_snd.at[k], head_rcv.at[frm], head=frm).wait_recv()
    parts = [hx[p].astype(F32) for p in range(H)]
    for q in range(S):
        lhs[:, q * DS:(q + 1) * DS] = jnp.concatenate(
            [part[q * R:(q + 1) * R] for part in parts], axis=0
        ).astype(BF16)
    loads[5].wait()
    A = wo.shape[0]
    AT = min(A, 512)
    for a0 in range(0, A, AT):
        head[:, a0:a0 + AT] = dot_nt(lhs[...], wo[a0:a0 + AT, :]).astype(BF16)
    for copy in sent:
        copy.wait_send()


def publish(resid, head, resid_out, head_out, sem):
    copies = [
        pltpu.make_async_copy(resid, resid_out, sem.at[0]),
        pltpu.make_async_copy(head, head_out, sem.at[1]),
    ]
    for copy in copies:
        copy.start()
    for copy in copies:
        copy.wait()


def shards(
    out_grad, layer_input, norm_gain, routes, gates, gate_pre, up_pre, w_gate, w_up, w_down, w_out
):
    S, E, H = lax.axis_size("seq"), lax.axis_size("exp"), lax.axis_size("head")
    T, D = out_grad.shape
    J, F = w_down.shape[:2]
    C = gate_pre.shape[3]
    A = w_out.shape[0]
    Z = E // 2
    DS = D // S
    R = T // S
    TN = LANES
    NT = DS // TN
    gp = gate_pre.reshape(J, E * C, F)
    up = up_pre.reshape(J, E * C, F)
    vmem = pl.BlockSpec(memory_space=pltpu.VMEM)
    hbm = pl.BlockSpec(memory_space=pl.ANY)
    dma = pltpu.SemaphoreType.DMA
    scratch = [
        pltpu.VMEM((E, S, T, DS), BF16),
        pltpu.VMEM((E, 8, 128), F32),
        pltpu.VMEM((E, 8, 128), F32),
        pltpu.VMEM((J, E * C, F), BF16),
        pltpu.VMEM((J, E * C, F), BF16),
        pltpu.VMEM((J, D, F), BF16),
        pltpu.VMEM((J, D, F), BF16),
        pltpu.VMEM((J, F, D), BF16),
        pltpu.VMEM((A, D), BF16),
        pltpu.VMEM((J, E * T, F), F32),
        pltpu.VMEM((J, E * T, F), F32),
        pltpu.VMEM((J, E * T, F), BF16),
        pltpu.VMEM((J, E * T, F), BF16),
        pltpu.VMEM((NT, 2, S, Z, T, TN), BF16),
        pltpu.VMEM((NT, S, Z, T, TN), BF16),
        pltpu.VMEM((NT, S, Z, T, TN), BF16),
        pltpu.VMEM((NT, S, Z, T, TN), BF16),
        pltpu.VMEM((NT, Z, T, TN), BF16),
        pltpu.VMEM((NT, Z, T, TN), BF16),
        pltpu.VMEM((R, D), F32),
        pltpu.VMEM((R, D), F32),
        pltpu.VMEM((H, T, DS), BF16),
        pltpu.VMEM((H * R, D), BF16),
        dma((6,)), dma((Z,)), dma((Z, S)), dma((Z, S)), dma((E,)), dma((NT,)),
        dma((NT, S)), dma((NT, Z)), dma((H,)),
        dma((E, S)), dma((E,)), dma((NT,)), dma((NT, S)), dma((NT, Z)), dma((H,)),
    ]
    rows = E * T
    flops = 2 * rows * D * F * J * 3 + 2 * H * R * D * A
    resid, head = pl.pallas_call(
        functools.partial(kernel, (S, E, H, J, T, D, C)),
        out_shape=(
            jax.ShapeDtypeStruct((R, D), F32),
            jax.ShapeDtypeStruct((H * R, A), BF16),
        ),
        in_specs=[vmem] * 5 + [hbm] * 6,
        out_specs=(vmem, vmem),
        scratch_shapes=scratch,
        compiler_params=pltpu.CompilerParams(
            collective_id=0, has_side_effects=True, vmem_limit_bytes=56 * 1024 * 1024
        ),
        cost_estimate=pl.CostEstimate(
            flops=flops, bytes_accessed=2 * (3 * J * D * F + A * D), transcendentals=rows * F * J
        ),
    )(
        out_grad, layer_input, norm_gain[None, :], routes.T, gates.T, gp, up,
        w_gate, w_up, w_down, w_out,
    )
    resid, head = pl.pallas_call(
        publish,
        out_shape=(
            jax.ShapeDtypeStruct(resid.shape, F32),
            jax.ShapeDtypeStruct(head.shape, BF16),
        ),
        in_specs=[hbm, hbm],
        out_specs=(hbm, hbm),
        scratch_shapes=[dma((2,))],
    )(resid, head)
    return (resid[None], head[None])


def solution(mesh):
    placed = (
        P(("exp", "head"), None),
        P(("exp", "head"), None),
        P(),
        P(("exp", "head"), None),
        P(("exp", "head"), None),
        P("head", "exp", None, None, "seq"),
        P("head", "exp", None, None, "seq"),
        P("exp", None, "seq"),
        P("exp", None, "seq"),
        P("exp", "seq", None),
        P("head", None),
    )
    return jax.shard_map(
        shards,
        mesh=mesh,
        in_specs=placed,
        out_specs=(P("seq", ("exp", "head"), None), P("seq", "exp", "head")),
        check_vma=False,
    )
```

```python
import functools

import jax
import jax.numpy as jnp
from jax import lax
from jax.experimental import pallas as pl
from jax.experimental.pallas import tpu as pltpu
from jax.sharding import PartitionSpec as P

MESH = pl.DeviceIdType.MESH
F32 = jnp.float32
BF16 = jnp.bfloat16
NT_DIMS = (((1,), (1,)), ((), ()))
LANES = 128


def dot_nt(a, b):
    return lax.dot_general(a, b, NT_DIMS, preferred_element_type=F32)


def kernel(
    sizes,
    og, li, gain, routes, gates, gp_hbm, up_hbm, wg_hbm, wu_hbm, wd_hbm, wo_hbm,
    resid, head,
    xg, info_src, info_all, gp, up, wg, wu, wd, wo, coef_gate, coef_up, dgate, dup,
    mine, core_rx, sx, x_rx, sz, z_rx, moe, normed, hx, lhs,
    load_sem, z_snd, sib_snd, x_snd, info_snd, core_snd, xs_snd, zs_snd, head_snd,
    xg_rcv, info_rcv, core_rcv, xs_rcv, zs_rcv, head_rcv,
):
    S, E, H, J, T, D, C = sizes
    Z = E // 2
    DS = D // S
    R = T // S
    F = wd.shape[1]
    TN = LANES
    NT = DS // TN
    s = lax.axis_index("seq")
    e = lax.axis_index("exp")
    h = lax.axis_index("head")
    z = e // 2
    c = e % 2
    sib = z * 2 + (1 - c)

    def remote(src, dst, snd, rcv, **where):
        return pltpu.make_async_remote_copy(
            src_ref=src, dst_ref=dst, send_sem=snd, recv_sem=rcv,
            device_id=where, device_id_type=MESH,
        )

    def rows_of(ref):
        wide = ref[...].astype(F32)
        mine_rows = wide[:R]
        for p in range(1, S):
            mine_rows = jnp.where(s == p, wide[p * R:(p + 1) * R], mine_rows)
        return mine_rows

    barrier = pltpu.get_barrier_semaphore()
    for k in range(1, E):
        pl.semaphore_signal(barrier, inc=1, device_id={"exp": (e + k) % E}, device_id_type=MESH)
    for k in range(1, S):
        pl.semaphore_signal(barrier, inc=1, device_id={"seq": (s + k) % S}, device_id_type=MESH)
    for k in range(1, H):
        pl.semaphore_signal(barrier, inc=1, device_id={"head": (h + k) % H}, device_id_type=MESH)

    loads = [
        pltpu.make_async_copy(src, dst, load_sem.at[i])
        for i, (src, dst) in enumerate(
            ((gp_hbm, gp), (up_hbm, up), (wd_hbm, wd), (wg_hbm, wg), (wu_hbm, wu), (wo_hbm, wo))
        )
    ]
    for load in loads[:3]:
        load.start()
    for q in range(S):
        xg[e, q] = og[:, q * DS:(q + 1) * DS]

    X8 = E * 8
    XP = max(LANES, X8)
    line = lax.broadcasted_iota(jnp.int32, (X8, T), 0)
    kind = line % 8
    expert = (line // 8) * J + kind % J
    weight = jnp.zeros((X8, T), F32)
    member = jnp.zeros((X8, T), F32)
    for k in range(routes.shape[0]):
        hit = routes[k:k + 1, :] == expert
        weight = weight + jnp.where(hit, gates[k:k + 1, :], 0.0)
        member = jnp.where(hit, 1.0, member)
    earlier = (
        lax.broadcasted_iota(jnp.int32, (T, T), 0) < lax.broadcasted_iota(jnp.int32, (T, T), 1)
    ).astype(F32).astype(BF16)
    position = jnp.dot(member.astype(BF16), earlier, preferred_element_type=F32)
    info = jnp.where(kind < J, weight, jnp.where(member > 0.0, position, -1.0))
    info_src[...] = jnp.zeros((E, 8, LANES), F32)
    info_src[:, :, :T] = info.reshape(E, 8, T)
    info_all[e] = info_src[e]

    pl.semaphore_wait(barrier, E - 1 + S - 1 + H - 1)

    room = jnp.minimum(z, Z - 1 - z)
    longer = jnp.where(2 * z < Z, 1, -1)

    def nearest(k):
        both = (k + 1) // 2 * (1 if k % 2 else -1)
        return z + longer * jnp.where(k <= 2 * room, both, k - room)

    order = [z] + [nearest(k) for k in range(1, Z)]

    sent = []

    def start(copy):
        copy.start()
        sent.append(copy)

    def chunk(block, part, snd, **where):
        return remote(xg.at[block, part], xg.at[block, part], snd, xg_rcv.at[block, part], **where)

    for k in range(1, E):
        to = (e + k) % E
        start(remote(info_src.at[to], info_all.at[e], info_snd.at[k], info_rcv.at[e], exp=to))
    for k in range(1, Z):
        start(chunk(e, s, z_snd.at[k], exp=order[k] * 2 + c))
    for q in range(S):
        start(chunk(e, q, sib_snd.at[0, q], exp=sib))

    for load in loads[3:]:
        load.start()

    inputs = rows_of(li)
    inv_rms = lax.rsqrt(jnp.mean(inputs * inputs, axis=1, keepdims=True) + 1e-06)
    normed[...] = inputs * inv_rms

    for k in range(1, E):
        frm = (e + k) % E
        remote(info_src.at[frm], info_all.at[frm], info_snd.at[k], info_rcv.at[frm], exp=frm).wait_recv()
    loads[0].wait()
    loads[1].wait()

    def slot_values(experts):
        table = info_all[...].reshape(X8, LANES)
        if XP > X8:
            table = jnp.concatenate([table, jnp.zeros((XP - X8, LANES), F32)], axis=0)
        table = table.T
        slot = lax.broadcasted_iota(jnp.int32, (E * T, E * C), 1).astype(F32)
        for j in experts:
            gate_col = jnp.concatenate([table[:T, b * 8 + j:b * 8 + j + 1] for b in range(E)], axis=0)
            place = []
            for b in range(E):
                col = table[:T, b * 8 + J + j:b * 8 + J + j + 1]
                place.append(jnp.where(col >= 0.0, col + float(b * C), -1.0))
            place = jnp.concatenate(place, axis=0)
            pick = jnp.where(slot == place, 1.0, 0.0).astype(BF16)
            a = jnp.dot(pick, gp[j], preferred_element_type=F32)
            b = jnp.dot(pick, up[j], preferred_element_type=F32)
            sig = jax.nn.sigmoid(a)
            coef_gate[j] = gate_col * b * sig * (1.0 + a * (1.0 - sig))
            coef_up[j] = gate_col * a * sig

    slot_values(range(1))

    for k in range(1, Z):
        block = order[k] * 2 + c
        chunk(block, s, z_snd.at[k], exp=sib).wait_recv()
        for i in range(1, S):
            start(chunk(block, s, x_snd.at[k, i], seq=(s + i) % S))
        start(chunk(block, s, sib_snd.at[k, 0], exp=sib))

    slot_values(range(1, J))

    for k in range(1, Z):
        block = order[k] * 2 + c
        for i in range(1, S):
            part = (s + S - i) % S
            chunk(block, part, x_snd.at[k, i], exp=sib).wait_recv()
            start(chunk(block, part, sib_snd.at[k, i], exp=sib))

    for k in range(Z):
        block = order[k] * 2 + (1 - c)
        for i in range(S):
            part = (s + S - i) % S
            chunk(block, part, sib_snd.at[k, i], exp=sib).wait_recv()

    loads[2].wait()
    hidden = None
    for q in range(S):
        down = wd[:, :, q * DS:(q + 1) * DS].reshape(J * F, DS)
        term = dot_nt(xg[:, q].reshape(E * T, DS), down)
        hidden = term if hidden is None else hidden + term
    for j in range(J):
        here = hidden[:, j * F:(j + 1) * F]
        dgate[j] = (here * coef_gate[j]).astype(BF16)
        dup[j] = (here * coef_up[j]).astype(BF16)
    loads[3].wait()
    loads[4].wait()

    def core_copy(n):
        return remote(mine.at[n, 1 - c], core_rx.at[n], core_snd.at[n], core_rcv.at[n], exp=sib)

    def x_copy(n, i):
        to = (s + i) % S
        return remote(sx.at[n, to], x_rx.at[n, i], xs_snd.at[n, i], xs_rcv.at[n, i], seq=to)

    def z_copy(n, k):
        to = (z + k) % Z
        return remote(sz.at[n, to], z_rx.at[n, k], zs_snd.at[n, k], zs_rcv.at[n, k], exp=to * 2 + c)

    def stage_compute(n):
        bands = [slice(q * DS + n * TN, q * DS + (n + 1) * TN) for q in range(S)]

        def weights(ref, j):
            return jnp.concatenate([ref[j, band, :] for band in bands], axis=0)

        left = [ref[j] for j in range(J) for ref in (dgate, dup)]
        right = [weights(ref, j) for j in range(J) for ref in (wg, wu)]
        if F % LANES == 0:
            acc = dot_nt(jnp.concatenate(left, axis=1), jnp.concatenate(right, axis=1))
        else:
            acc = sum(dot_nt(lt, rt) for lt, rt in zip(left, right))
        tiles = [acc[:, q * TN:(q + 1) * TN] for q in range(S)]
        for b in range(E):
            for p in range(S):
                rows = slice(b * T + p * R, b * T + (p + 1) * R)
                mine[n, b % 2, p, b // 2] = jnp.concatenate(
                    [tile[rows] for tile in tiles], axis=0
                ).astype(BF16)
        start(core_copy(n))

    def stage_x(n):
        core_copy(n).wait_recv()
        sx[n] = (mine[n, c].astype(F32) + core_rx[n].astype(F32)).astype(BF16)
        for i in range(1, S):
            start(x_copy(n, i))

    def stage_z(n):
        total = sx[n, s].astype(F32)
        for i in range(1, S):
            x_copy(n, i).wait_recv()
            total = total + x_rx[n, i].astype(F32)
        sz[n] = total.astype(BF16)
        for k in range(1, Z):
            start(z_copy(n, k))

    def stage_end(n):
        total = sz[n, z].astype(F32)
        for k in range(1, Z):
            z_copy(n, k).wait_recv()
            total = total + z_rx[n, k].astype(F32)
        for q in range(S):
            moe[:, q * DS + n * TN:q * DS + (n + 1) * TN] = total[q * R:(q + 1) * R]

    for n in range(NT):
        stage_compute(n)
        if n >= 1:
            stage_x(n - 1)
        if n >= 5:
            stage_z(n - 5)
    stage_x(NT - 1)
    for n in range(max(NT - 5, 0), NT):
        stage_z(n)
    for n in range(NT):
        stage_end(n)

    scaled = moe[...] * gain[...]
    full = rows_of(og) + inv_rms * (
        scaled - normed[...] * jnp.mean(scaled * normed[...], axis=1, keepdims=True)
    )
    resid[...] = full
    hx[h] = jnp.concatenate([full[:, q * DS:(q + 1) * DS] for q in range(S)], axis=0).astype(BF16)
    for k in range(1, H):
        start(remote(hx.at[h], hx.at[h], head_snd.at[k], head_rcv.at[h], head=(h + k) % H))
    for k in range(1, H):
        frm = (h + k) % H
        remote(hx.at[frm], hx.at[frm], head_snd.at[k], head_rcv.at[frm], head=frm).wait_recv()
    parts = [hx[p].astype(F32) for p in range(H)]
    for q in range(S):
        lhs[:, q * DS:(q + 1) * DS] = jnp.concatenate(
            [part[q * R:(q + 1) * R] for part in parts], axis=0
        ).astype(BF16)
    loads[5].wait()
    A = wo.shape[0]
    AT = min(A, 512)
    for a0 in range(0, A, AT):
        head[:, a0:a0 + AT] = dot_nt(lhs[...], wo[a0:a0 + AT, :]).astype(BF16)
    for copy in sent:
        copy.wait_send()


def publish(resid, head, resid_out, head_out, resid_v, head_v, sem):
    arrive = [
        pltpu.make_async_copy(head, head_v, sem.at[0]),
        pltpu.make_async_copy(resid, resid_v, sem.at[1]),
    ]
    leave = [
        pltpu.make_async_copy(head_v, head_out, sem.at[2]),
        pltpu.make_async_copy(resid_v, resid_out, sem.at[3]),
    ]
    for copy in arrive:
        copy.start()
    for first, second in zip(arrive, leave):
        first.wait()
        second.start()
    for copy in leave:
        copy.wait()


def shards(
    out_grad, layer_input, norm_gain, routes, gates, gate_pre, up_pre, w_gate, w_up, w_down, w_out
):
    S, E, H = lax.axis_size("seq"), lax.axis_size("exp"), lax.axis_size("head")
    T, D = out_grad.shape
    J, F = w_down.shape[:2]
    C = gate_pre.shape[3]
    A = w_out.shape[0]
    Z = E // 2
    DS = D // S
    R = T // S
    TN = LANES
    NT = DS // TN
    gp = gate_pre.reshape(J, E * C, F)
    up = up_pre.reshape(J, E * C, F)
    vmem = pl.BlockSpec(memory_space=pltpu.VMEM)
    hbm = pl.BlockSpec(memory_space=pl.ANY)
    dma = pltpu.SemaphoreType.DMA
    scratch = [
        pltpu.VMEM((E, S, T, DS), BF16),
        pltpu.VMEM((E, 8, 128), F32),
        pltpu.VMEM((E, 8, 128), F32),
        pltpu.VMEM((J, E * C, F), BF16),
        pltpu.VMEM((J, E * C, F), BF16),
        pltpu.VMEM((J, D, F), BF16),
        pltpu.VMEM((J, D, F), BF16),
        pltpu.VMEM((J, F, D), BF16),
        pltpu.VMEM((A, D), BF16),
        pltpu.VMEM((J, E * T, F), F32),
        pltpu.VMEM((J, E * T, F), F32),
        pltpu.VMEM((J, E * T, F), BF16),
        pltpu.VMEM((J, E * T, F), BF16),
        pltpu.VMEM((NT, 2, S, Z, T, TN), BF16),
        pltpu.VMEM((NT, S, Z, T, TN), BF16),
        pltpu.VMEM((NT, S, Z, T, TN), BF16),
        pltpu.VMEM((NT, S, Z, T, TN), BF16),
        pltpu.VMEM((NT, Z, T, TN), BF16),
        pltpu.VMEM((NT, Z, T, TN), BF16),
        pltpu.VMEM((R, D), F32),
        pltpu.VMEM((R, D), F32),
        pltpu.VMEM((H, T, DS), BF16),
        pltpu.VMEM((H * R, D), BF16),
        dma((6,)), dma((Z,)), dma((Z, S)), dma((Z, S)), dma((E,)), dma((NT,)),
        dma((NT, S)), dma((NT, Z)), dma((H,)),
        dma((E, S)), dma((E,)), dma((NT,)), dma((NT, S)), dma((NT, Z)), dma((H,)),
    ]
    rows = E * T
    flops = 2 * rows * D * F * J * 3 + 2 * H * R * D * A
    resid, head = pl.pallas_call(
        functools.partial(kernel, (S, E, H, J, T, D, C)),
        out_shape=(
            jax.ShapeDtypeStruct((R, D), F32),
            jax.ShapeDtypeStruct((H * R, A), BF16),
        ),
        in_specs=[vmem] * 5 + [hbm] * 6,
        out_specs=(vmem, vmem),
        scratch_shapes=scratch,
        compiler_params=pltpu.CompilerParams(
            collective_id=0, has_side_effects=True, vmem_limit_bytes=56 * 1024 * 1024
        ),
        cost_estimate=pl.CostEstimate(
            flops=flops, bytes_accessed=2 * (3 * J * D * F + A * D), transcendentals=rows * F * J
        ),
    )(
        out_grad, layer_input, norm_gain[None, :], routes.T, gates.T, gp, up,
        w_gate, w_up, w_down, w_out,
    )
    resid, head = pl.pallas_call(
        publish,
        out_shape=(
            jax.ShapeDtypeStruct(resid.shape, F32),
            jax.ShapeDtypeStruct(head.shape, BF16),
        ),
        in_specs=[hbm, hbm],
        out_specs=(hbm, hbm),
        scratch_shapes=[
            pltpu.VMEM(resid.shape, F32), pltpu.VMEM(head.shape, BF16), dma((4,))
        ],
    )(resid, head)
    return (resid[None], head[None])


def solution(mesh):
    placed = (
        P(("exp", "head"), None),
        P(("exp", "head"), None),
        P(),
        P(("exp", "head"), None),
        P(("exp", "head"), None),
        P("head", "exp", None, None, "seq"),
        P("head", "exp", None, None, "seq"),
        P("exp", None, "seq"),
        P("exp", None, "seq"),
        P("exp", "seq", None),
        P("head", None),
    )
    return jax.shard_map(
        shards,
        mesh=mesh,
        in_specs=placed,
        out_specs=(P("seq", ("exp", "head"), None), P("seq", "exp", "head")),
        check_vma=False,
    )
```
